512 devices in a mesh: replica: 16 (over z_hi, x), fsdp: 32 (over y, z_lo, core).
Axes of the slice: x: 4, y: 4, z: 16 (z_hi: 4, z_lo: 4; z = z_hi * 4 + z_lo), core: 2. Of those that a mesh axis runs over, the one named last changes fastest.
Arguments:
- acts: bfloat16 [65536, 8192], P(('replica', 'fsdp')), may hold values from -24 to 24
- norm_gain: float32 [8192], replicated, may hold values from 0.5 to 1.5
- cotangent: bfloat16 [65536, 512], P(('replica', 'fsdp')), may hold values from -0.59765625 to 0.59765625
- inner_weight: float32 [16, 8192, 512], P('replica', 'fsdp'), may hold values from -0.18 to 0.18
- first_moment: bfloat16 [16, 8192, 512], P('replica', 'fsdp'), may hold values from -6 to 6
- second_moment: bfloat16 [16, 8192, 512], P('replica', 'fsdp'), may hold values from 0.049804688 to 5
- local_fragment: float32 [16, 8192, 512], P('replica', 'fsdp'), may hold values from -0.0625 to 0.0625
- global_fragment: float32 [8192, 512], P('fsdp', 'replica'), may hold values from -0.0625 to 0.0625
- outer_momentum: float32 [8192, 512], P('fsdp', 'replica'), may hold values from -0.06 to 0.06
Outputs:
- new_weight: float32 [16, 8192, 512], P('replica', 'fsdp')
- new_first_moment: bfloat16 [16, 8192, 512], P('replica', 'fsdp')
- new_second_moment: bfloat16 [16, 8192, 512], P('replica', 'fsdp')
- new_global: float32 [8192, 512], P('fsdp', 'replica')
- new_momentum: float32 [8192, 512], P('fsdp', 'replica')
- next_features: bfloat16 [65536, 512], P(('replica', 'fsdp'))
The draws below stay inside these ranges and needn't reach their ends.
All inputs are finite; a program needn't handle non-finite values.
Results may differ from the reference program's by a relative error of at most 0.0058.
Values may be sent and summed in bfloat16 or wider, within the bound.
A program may use at most 64 MiB of HBM per device.

```python
import math
import jax
import jax.numpy as jnp
from jax import lax

D = 8192
KW = 512
FRAG = 512
TOK_DEV = 128
GROUPS = 16
TOKENS = 65536
N_REPLICA = 16
N_FSDP = 32


def strengthened(entries, stream_key, source, target, shards_of, factor):
    def block_of(position):
        return (jnp.arange(entries.shape[position]) // (entries.shape[position] // shards_of)).reshape((-1,) + (1,) * (entries.ndim - 1 - position))

    one_side = jax.random.permutation(stream_key, shards_of)[block_of(target)]
    other_side = (block_of(target) + shards_of // 2) % shards_of
    return jnp.where((block_of(source) == one_side) | (block_of(source) == other_side), factor * entries, entries)


def block_levels(key, extent, split, least, largest):
    def one(position, blocks):
        heights = jax.random.uniform(jax.random.fold_in(jax.random.fold_in(key, 6), position), (blocks,), jnp.float32, least / len(split), largest / len(split))
        return jnp.repeat(jnp.exp(heights), extent[position] // blocks).reshape((-1,) + (1,) * (len(extent) - position - 1))

    level = one(*split[0])
    for cut in split[1:]:
        level = level * one(*cut)
    return level


def noise(key, extent, spread, reach, split=(), dtype=jnp.bfloat16):
    values = spread * jax.random.normal(key, extent, jnp.float32)
    if split:
        values = values * block_levels(key, extent, split, -0.22, 0.18)
    return jnp.clip(values, -reach, reach).astype(dtype)


def gaussian_with(own_key, extent, scale, reach, split, heavy, kind=jnp.bfloat16):
    values = scale * jax.random.normal(own_key, extent, jnp.float32)
    if split:
        values = values * block_levels(own_key, extent, split, -0.22, 0.18)
    return jnp.clip(strengthened(values, jax.random.fold_in(own_key, 3), *heavy), -reach, reach).astype(kind)


def setup_inputs(seed: int = 0) -> dict:
    splits = jax.random.split(jax.random.key(seed), 10)
    return {
        "acts": gaussian_with(splits[0], (TOKENS, D), 1.0, 24.0, ((0, 512),), (0, 1, 512, 6.0)),
        "norm_gain": jnp.clip(1.0 + 0.1 * jax.random.normal(splits[1], (D,), jnp.float32), 0.5, 1.5),
        "cotangent": noise(splits[2], (TOKENS, KW), 0.1, 0.59765625, ((0, 512),)),
        "inner_weight": noise(splits[3], (GROUPS, D, KW), 0.03, 0.18, ((0, 16), (1, 32)), jnp.float32),
        "first_moment": noise(splits[4], (GROUPS, D, KW), 1.0, 6.0, ((0, 16), (1, 32))),
        "second_moment": jnp.clip(jnp.exp(math.log(5.0) - 4.609084 * jax.random.uniform(splits[5], (GROUPS, D, KW), jnp.float32) ** block_levels(splits[5], (GROUPS, D, KW), ((0, 16), (1, 32)), -0.2, 0.2)), 0.049804688, 5.0).astype(jnp.bfloat16),
        "local_fragment": noise(splits[6], (GROUPS, D, FRAG), D ** -0.5, 0.0625, ((0, 16), (1, 32)), jnp.float32),
        "global_fragment": noise(splits[7], (D, FRAG), D ** -0.5, 0.0625, ((0, 32), (1, 16)), jnp.float32),
        "outer_momentum": noise(splits[8], (D, FRAG), 0.01, 0.06, ((0, 32), (1, 16)), jnp.float32),
    }


beta_one = 0.9
beta_two = 0.95
adam_epsilon = 1e-08
inner_rate = 0.01
weight_decay = 0.1
bias_first = 1.0 - 0.9 ** 20
bias_second = 1.0 - 0.95 ** 20
outer_rate = 0.7
outer_beta = 0.9
norm_epsilon = 1e-05

def normalize(rows, norm_gain):
    full = rows.astype(jnp.float32)
    rstd = lax.rsqrt(lax.optimization_barrier(jnp.mean(full * full, axis=1, keepdims=True)) + norm_epsilon)
    return (full * rstd * norm_gain[None, :]).astype(jnp.bfloat16)

def reference(acts, norm_gain, cotangent, inner_weight, first_moment, second_moment, local_fragment, global_fragment, outer_momentum):
    mean_delta = global_fragment - lax.optimization_barrier(jnp.sum(local_fragment, axis=0)) / N_REPLICA
    new_momentum = outer_beta * outer_momentum + mean_delta
    new_global = global_fragment - outer_rate * (mean_delta + outer_beta * new_momentum)
    narrow = new_global.astype(jnp.bfloat16)
    xs = acts.reshape(N_REPLICA, N_FSDP * TOK_DEV, D)
    ds = cotangent.reshape(N_REPLICA, N_FSDP * TOK_DEV, KW)

    def group_work(pair):
        rows, cots = pair
        normed = normalize(rows, norm_gain)
        grad = jnp.dot(normed.T, cots, preferred_element_type=jnp.float32)
        feats = jnp.dot(normed, narrow, preferred_element_type=jnp.float32).astype(jnp.bfloat16)
        return (grad, feats)
    grad, feats = lax.map(group_work, (xs, ds))
    first = beta_one * first_moment.astype(jnp.float32) + (1.0 - beta_one) * grad
    second = beta_two * second_moment.astype(jnp.float32) + (1.0 - beta_two) * grad * grad
    ratio = first / bias_first / (jnp.sqrt(second / bias_second) + adam_epsilon)
    new_weight = inner_weight - inner_rate * (ratio + weight_decay * inner_weight)
    next_features = feats.reshape(N_REPLICA * N_FSDP * TOK_DEV, FRAG)
    return (new_weight, first.astype(jnp.bfloat16), second.astype(jnp.bfloat16), new_global, new_momentum, next_features)
```

```python
import functools

import jax
import jax.numpy as jnp
from jax import lax
from jax.experimental import pallas as pl
from jax.experimental.pallas import tpu as pltpu
from jax.sharding import PartitionSpec as P

beta_one = 0.9
beta_two = 0.95
adam_epsilon = 1e-08
inner_rate = 0.01
weight_decay = 0.1
bias_first = 1.0 - 0.9**20
bias_second = 1.0 - 0.95**20
outer_rate = 0.7
outer_beta = 0.9
norm_epsilon = 1e-05

MESH = pl.DeviceIdType.MESH
F32 = jnp.float32
BF16 = jnp.bfloat16


def kernel(
    acts_h, gain_h, cot_h, w_h, fm_h, sm_h, lf_h, g_h, m_h,
    w_o, fm_o, sm_o, ng_o, nm_o, ft_o,
    acts, gain, normed, cot, w, fm, sm, lf, g, m,
    lt, lr, part, pr, nt, xs, gsend, gown, grecv, zsend, zrecv, fsend, frecv,
    lsem, xsem, csem_s, csem_r, asem_s, asem_r,
    lsem_s, lsem_r, psem_s, psem_r, hsem_s, hsem_r,
    t2sem_s, t2sem_r, t3sem_s, t3sem_r, dsem_s, dsem_r,
    gsem_s, gsem_r, zsem_s, zsem_r, fsem_s, fsem_r,
):
    rep = lax.axis_index("replica")
    fs = lax.axis_index("fsdp")
    zh, x = rep // 4, lax.rem(rep, 4)
    y, zl, c = fs // 8, lax.rem(fs // 2, 4), lax.rem(fs, 2)
    z = zh * 4 + zl

    def at(zh=zh, x=x, y=y, zl=zl, c=c):
        return (zh * 4 + x, y * 8 + zl * 2 + c)

    def at_z(zz):
        return at(zh=zz // 4, zl=lax.rem(zz, 4))

    def turn(value, step, size):
        return lax.rem(value + step + size, size)

    def send(src, dst, ss, rs, device):
        copy = pltpu.make_async_remote_copy(
            src_ref=src, dst_ref=dst, send_sem=ss, recv_sem=rs,
            device_id=device, device_id_type=MESH,
        )
        copy.start()
        return copy

    other = at(c=1 - c)
    skew = 2 - 4 * lax.rem(zl, 2)
    flips = (3 - zl, lax.rem(zl + 2, 4), zl + 1 - 2 * lax.rem(zl, 2), zl)

    loads = []
    for i, (src, dst) in enumerate((
        (lf_h, lf), (acts_h, acts), (gain_h, gain),
        (cot_h, cot.at[pl.ds(pl.multiple_of(y * 128, 128), 128)]),
        (g_h, g), (m_h, m), (w_h, w), (fm_h, fm), (sm_h, sm),
    )):
        copy = pltpu.make_async_copy(src, dst, lsem.at[i])
        copy.start()
        loads.append(copy)

    barrier = pltpu.get_barrier_semaphore()
    sources = [other]
    sources += [at(y=turn(y, d, 4)) for d in (1, 2, 3)]
    sources += [at(x=turn(x, d, 4)) for d in (1, 2, 3)]
    sources += [at(zh=turn(zh, d, 4)) for d in (1, 2, 3)]
    sources += [at(zl=flips[s]) for s in range(3)]
    sources += [at_z(turn(z, 1, 16)), at_z(turn(z, -1, 16)), at_z(turn(z, -skew, 16))]
    for device in sources:
        pl.semaphore_signal(barrier, inc=1, device_id=device, device_id_type=MESH)

    loads[0].wait()
    for k in range(4):
        turned = lf[:, k * 128:(k + 1) * 128].T
        for j in range(4):
            lt[j, k] = turned[j * 32:(j + 1) * 32]

    loads[1].wait()
    loads[2].wait()

    def norm_rows(i, carry):
        rows = pl.ds(pl.multiple_of(i * 16, 16), 16)
        full = acts[rows, :].astype(F32)
        rstd = lax.rsqrt(jnp.sum(full * full, axis=1, keepdims=True) / 8192.0 + norm_epsilon)
        normed[rows, :] = (full * rstd * gain[...]).astype(BF16)
        return carry

    lax.fori_loop(0, 8, norm_rows, 0)
    loads[3].wait()

    pl.semaphore_wait(barrier, len(sources))

    sends = []
    for i, d in enumerate((1, 3, 2)):
        to = turn(x, d, 4)
        sends.append(send(lt.at[to], lr.at[i], lsem_s.at[i], lsem_r.at[i], at(x=to)))
    along_x = sends[-3:]
    mine = pl.ds(pl.multiple_of(y * 128, 128), 128)
    for i, d in enumerate((1, 3, 2)):
        sends.append(send(cot.at[mine], cot.at[mine], csem_s.at[i], csem_r.at[i], at(y=turn(y, d, 4))))
    cots = sends[-3:]
    chunks, keeps = [], []
    for s in range(4):
        row = []
        for i, d in enumerate((1, 3, 2)):
            to = turn(y, d, 4)
            cols = pl.ds(pl.multiple_of(to * 2048 + flips[s] * 512, 512), 512)
            row.append(send(normed.at[:, cols], xs.at[s, mine], asem_s.at[s * 3 + i], asem_r.at[s * 3 + i], at(y=to)))
        cols = pl.ds(pl.multiple_of(y * 2048 + flips[s] * 512, 512), 512)
        keep = pltpu.make_async_copy(normed.at[:, cols], xs.at[s, mine], xsem.at[s])
        keep.start()
        keeps.append(keep)
        chunks.append(row)
        sends += row

    def sum_x():
        for copy in along_x:
            copy.wait_recv()
        part[...] = lt[x] + lr[0] + lr[1] + lr[2]
        out = []
        for i, d in enumerate((1, 3, 2)):
            to = turn(zh, d, 4)
            out.append(send(part.at[to], pr.at[i], psem_s.at[i], psem_r.at[i], at(zh=to)))
        return out

    def outer_update(copies):
        for copy in copies:
            copy.wait_recv()
        loads[4].wait()
        loads[5].wait()
        total = part[zh] + pr[0] + pr[1] + pr[2]
        mean_delta = g[...] - total / 16.0
        new_momentum = outer_beta * m[...] + mean_delta
        new_global = g[...] - outer_rate * (mean_delta + outer_beta * new_momentum)
        ng_o[...] = new_global
        nm_o[...] = new_momentum
        nt[zl, c, zh, x] = new_global.astype(BF16)
        out = []
        for i, d in enumerate((1, 3, 2)):
            piece = nt.at[zl, c, zh, x]
            out.append(send(piece, piece, hsem_s.at[i], hsem_r.at[i], at(zh=turn(zh, d, 4))))
        return out

    x_peers = [at(x=turn(x, d, 4)) for d in (1, 3, 2)]
    z_peers = [at_z(turn(z, 1, 16)), at_z(turn(z, -1, 16)), at_z(turn(z, skew, 16))]

    def gather_two(copies):
        for copy in copies:
            copy.wait_recv()
        out = []
        for i in range(3):
            piece = nt.at[zl, c, pl.ds(0, 2), x]
            out.append(send(piece, piece, t2sem_s.at[i], t2sem_r.at[i], x_peers[i]))
            piece = nt.at[zl, c, pl.ds(2, 2), x]
            out.append(send(piece, piece, t2sem_s.at[3 + i], t2sem_r.at[3 + i], z_peers[i]))
        return out

    def gather_three(copies):
        for copy in copies:
            copy.wait_recv()
        out = []
        for i in range(3):
            piece = nt.at[zl, c, pl.ds(0, 2)]
            out.append(send(piece, piece, t3sem_s.at[i], t3sem_r.at[i], z_peers[i]))
            piece = nt.at[:, c, pl.ds(2, 2), x]
            out.append(send(piece, piece, t3sem_s.at[3 + i], t3sem_r.at[3 + i], x_peers[i]))
        return out

    def gather_core(copies):
        for copy in copies:
            copy.wait_recv()
        piece = nt.at[:, c]
        return [send(piece, piece, dsem_s.at[0], dsem_r.at[0], other)]

    def half(core):
        return pl.ds(pl.multiple_of(core * 256, 256), 256)

    def grad_of(s, core):
        return lax.dot_general(
            xs[s, :, half(core)], cot[...], (((0,), (0,)), ((), ())), preferred_element_type=F32
        )

    def chunk_in(s):
        for copy in chunks[s]:
            copy.wait_recv()
        keeps[s].wait()
        gsend[s] = grad_of(s, 1 - c)
        copy = send(gsend.at[s], grecv.at[s], gsem_s.at[s], gsem_r.at[s], other)
        gown[s] = grad_of(s, c)
        return copy

    def chunk_out(s, copy):
        copy.wait_recv()
        zsend[s] = (gown[s] + grecv[s]).astype(BF16)
        return send(zsend.at[s], zrecv.at[s], zsem_s.at[s], zsem_r.at[s], at(zl=flips[s]))

    def feature_part(core):
        total = None
        for s in range(4):
            rows = nt[flips[s], core].reshape(512, 256)
            term = lax.dot_general(
                xs[s, :, half(core)], rows, (((1,), (1,)), ((), ())), preferred_element_type=F32
            )
            total = term if total is None else total + term
        return total

    pcopies = sum_x()
    for copy in cots:
        copy.wait_recv()
    hcopies = outer_update(pcopies)
    g0 = chunk_in(0)
    t2 = gather_two(hcopies)
    z0 = chunk_out(0, g0)
    g1 = chunk_in(1)
    t3 = gather_three(t2)
    z1 = chunk_out(1, g1)
    g2 = chunk_in(2)
    z2 = chunk_out(2, g2)
    dcopies = gather_core(t3)
    g3 = chunk_in(3)
    fpart = feature_part(c)
    for copy in dcopies:
        copy.wait_recv()
    fpart = fpart + feature_part(1 - c)
    for k in range(4):
        fsend[k] = fpart[k * 128:(k + 1) * 128]
    fb = frecv.at[3]
    fcopies = []
    for i, d in enumerate((1, 3, 2)):
        to = turn(y, d, 4)
        frecv[4 + i] = fsend[to].astype(BF16)
        fcopies.append(send(frecv.at[4 + i], frecv.at[i], fsem_s.at[i], fsem_r.at[i], at(y=to)))

    g3.wait_recv()
    for i in (6, 7, 8):
        loads[i].wait()
    for copy in (z0, z1, z2):
        copy.wait_recv()
    grad = gown[3] + grecv[3] + zrecv[0].astype(F32) + zrecv[1].astype(F32) + zrecv[2].astype(F32)
    first = beta_one * fm[...].astype(F32) + (1.0 - beta_one) * grad
    second = beta_two * sm[...].astype(F32) + (1.0 - beta_two) * grad * grad
    ratio = first / bias_first / (jnp.sqrt(second / bias_second) + adam_epsilon)
    w_o[...] = w[...] - inner_rate * (ratio + weight_decay * w[...])
    fm_o[...] = first.astype(BF16)
    sm_o[...] = second.astype(BF16)

    for copy in fcopies:
        copy.wait_recv()
    ft_o[...] = (
        fsend[y] + frecv[0].astype(F32) + frecv[1].astype(F32) + frecv[2].astype(F32)
    ).astype(BF16)

    for copy in sends + pcopies + hcopies + t2 + t3 + dcopies + [g0, g1, g2, g3, z0, z1, z2] + fcopies:
        copy.wait_send()


def body(
    acts,
    norm_gain,
    cotangent,
    inner_weight,
    first_moment,
    second_moment,
    local_fragment,
    global_fragment,
    outer_momentum,
):
    vmem, anywhere = pl.BlockSpec(memory_space=pltpu.VMEM), pl.BlockSpec(memory_space=pl.ANY)
    dma = pltpu.SemaphoreType.DMA
    outs = pl.pallas_call(
        kernel,
        out_shape=(
            jax.ShapeDtypeStruct((256, 512), F32),
            jax.ShapeDtypeStruct((256, 512), BF16),
            jax.ShapeDtypeStruct((256, 512), BF16),
            jax.ShapeDtypeStruct((32, 256), F32),
            jax.ShapeDtypeStruct((32, 256), F32),
            jax.ShapeDtypeStruct((128, 512), BF16),
        ),
        in_specs=[anywhere] * 9,
        out_specs=[vmem] * 6,
        scratch_shapes=[
            pltpu.VMEM((128, 8192), BF16),
            pltpu.VMEM((1, 8192), F32),
            pltpu.VMEM((128, 8192), BF16),
            pltpu.VMEM((512, 512), BF16),
            pltpu.VMEM((256, 512), F32),
            pltpu.VMEM((256, 512), BF16),
            pltpu.VMEM((256, 512), BF16),
            pltpu.VMEM((256, 512), F32),
            pltpu.VMEM((32, 256), F32),
            pltpu.VMEM((32, 256), F32),
            pltpu.VMEM((4, 4, 32, 256), F32),
            pltpu.VMEM((3, 4, 32, 256), F32),
            pltpu.VMEM((4, 32, 256), F32),
            pltpu.VMEM((3, 32, 256), F32),
            pltpu.VMEM((4, 2, 4, 4, 32, 256), BF16),
            pltpu.VMEM((4, 512, 512), BF16),
            pltpu.VMEM((4, 256, 512), F32),
            pltpu.VMEM((4, 256, 512), F32),
            pltpu.VMEM((4, 256, 512), F32),
            pltpu.VMEM((3, 256, 512), BF16),
            pltpu.VMEM((3, 256, 512), BF16),
            pltpu.VMEM((4, 128, 512), F32),
            pltpu.VMEM((7, 128, 512), BF16),
            dma((9,)), dma((4,)), dma((3,)), dma((3,)), dma((12,)), dma((12,)),
            dma((3,)), dma((3,)), dma((3,)), dma((3,)), dma((3,)), dma((3,)),
            dma((6,)), dma((6,)), dma((6,)), dma((6,)), dma((1,)), dma((1,)),
            dma((4,)), dma((4,)), dma((3,)), dma((3,)), dma((3,)), dma((3,)),
        ],
        compiler_params=pltpu.CompilerParams(
            collective_id=0, has_side_effects=True, vmem_limit_bytes=63 * 2**20
        ),
        name="window_step",
    )(
        acts, norm_gain[None], cotangent, inner_weight[0], first_moment[0], second_moment[0],
        local_fragment[0], global_fragment.T, outer_momentum.T,
    )
    new_weight, new_first, new_second, new_global, new_momentum, features = outs
    return (new_weight[None], new_first[None], new_second[None], new_global.T, new_momentum.T, features)


def solution(mesh):
    placed = (
        P(("replica", "fsdp"), None),
        P(),
        P(("replica", "fsdp"), None),
        P("replica", "fsdp", None),
        P("replica", "fsdp", None),
        P("replica", "fsdp", None),
        P("replica", "fsdp", None),
        P("fsdp", "replica"),
        P("fsdp", "replica"),
    )
    return jax.shard_map(
        body,
        mesh=mesh,
        in_specs=placed,
        out_specs=(
            P("replica", "fsdp", None),
            P("replica", "fsdp", None),
            P("replica", "fsdp", None),
            P("fsdp", "replica"),
            P("fsdp", "replica"),
            P(("replica", "fsdp"), None),
        ),
        check_vma=False,
    )
```

```python
import functools

import jax
import jax.numpy as jnp
from jax import lax
from jax.experimental import pallas as pl
from jax.experimental.pallas import tpu as pltpu
from jax.sharding import PartitionSpec as P

beta_one = 0.9
beta_two = 0.95
adam_epsilon = 1e-08
inner_rate = 0.01
weight_decay = 0.1
bias_first = 1.0 - 0.9**20
bias_second = 1.0 - 0.95**20
outer_rate = 0.7
outer_beta = 0.9
norm_epsilon = 1e-05

MESH = pl.DeviceIdType.MESH
F32 = jnp.float32
BF16 = jnp.bfloat16


def kernel(
    acts_h, gain_h, cot_h, w_h, fm_h, sm_h, lf_h, g_h, m_h,
    w_o, fm_o, sm_o, ng_o, nm_o, ft_o,
    acts, gain, normed, cot, w, fm, sm, lf, g, m,
    lt, lr, part, pr, nt, xs, gsend, gown, grecv, zsend, zrecv, fown, fsend, frecv,
    load_sem, keep_sem, vouch,
    cot_s, cot_r, tok_s, tok_r, along_s, along_r, far_s, far_r, gat_s, gat_r,
    line_s, line_r, wide_s, wide_r, core_s, core_r,
    grad_s, grad_r, z_s, z_r, feat_s, feat_r,
):
    rep = lax.axis_index("replica")
    fs = lax.axis_index("fsdp")
    zh, x = rep // 4, lax.rem(rep, 4)
    y, zl, c = fs // 8, lax.rem(fs // 2, 4), lax.rem(fs, 2)
    z = zh * 4 + zl

    def at(zh=zh, x=x, y=y, zl=zl, c=c):
        return (zh * 4 + x, y * 8 + zl * 2 + c)

    def at_z(zz):
        return at(zh=zz // 4, zl=lax.rem(zz, 4))

    def turn(value, step, size=4):
        return lax.rem(value + step + size, size)

    sends = []

    def send(src, dst, ss, rs, device):
        copy = pltpu.make_async_remote_copy(
            src_ref=src, dst_ref=dst, send_sem=ss, recv_sem=rs,
            device_id=device, device_id_type=MESH,
        )
        copy.start()
        sends.append(copy)
        return copy

    def signal(sem, device):
        pl.semaphore_signal(sem, inc=1, device_id=device, device_id_type=MESH)

    other = at(c=1 - c)
    steps = (1, 3, 2)
    x_peers = [at(x=turn(x, d)) for d in steps]
    y_peers = [at(y=turn(y, d)) for d in steps]
    skew = 2 - 4 * lax.rem(zl, 2)
    z_peers = [at_z(turn(z, 1, 16)), at_z(turn(z, -1, 16)), at_z(turn(z, skew, 16))]
    z_from = (turn(zl, -1), turn(zl, 1), turn(zl, 2))
    flips = (3 - zl, turn(zl, 2), zl + 1 - 2 * lax.rem(zl, 2), zl)
    middle = (zl * (3 - zl)) // 2

    loads = []
    for i, (src, dst) in enumerate((
        (lf_h, lf), (acts_h, acts), (gain_h, gain),
        (cot_h, cot.at[pl.ds(pl.multiple_of(y * 128, 128), 128)]),
        (g_h, g), (m_h, m), (w_h, w), (fm_h, fm), (sm_h, sm),
    )):
        copy = pltpu.make_async_copy(src, dst, load_sem.at[i])
        copy.start()
        loads.append(copy)

    barrier = pltpu.get_barrier_semaphore()
    near = [other] + x_peers + y_peers
    near += [at(zl=flips[s]) for s in range(3)]
    near += [at_z(turn(z, d, 16)) for d in (1, -1, 2, -2)]
    for device in near:
        signal(barrier, device)

    loads[0].wait()
    for k in range(4):
        turned = lf[:, k * 128:(k + 1) * 128].T
        for j in range(4):
            lt[j, k] = turned[j * 32:(j + 1) * 32]
    loads[3].wait()

    pl.semaphore_wait(barrier, len(near))

    far = [turn(zh, d) for d in (2, 1, 3, 0)]
    along = []
    for k in range(4):
        along.append([
            send(lt.at[turn(x, d), far[k]], lr.at[i, k], along_s.at[k * 3 + i], along_r.at[k * 3 + i], x_peers[i])
            for i, d in enumerate(steps)
        ])
    mine = pl.ds(pl.multiple_of(y * 128, 128), 128)
    cots = [send(cot.at[mine], cot.at[mine], cot_s.at[i], cot_r.at[i], y_peers[i]) for i in range(3)]
    for d in (2, -2):
        signal(vouch.at[0], at_z(turn(z, d, 16)))

    loads[1].wait()
    loads[2].wait()

    def norm_rows(i, carry):
        rows = pl.ds(pl.multiple_of(i * 16, 16), 16)
        full = acts[rows, :].astype(F32)
        rstd = lax.rsqrt(jnp.sum(full * full, axis=1, keepdims=True) / 8192.0 + norm_epsilon)
        normed[rows, :] = (full * rstd * gain[...]).astype(BF16)
        return carry

    lax.fori_loop(0, 4, norm_rows, 0)
    pl.semaphore_wait(vouch.at[0], 2)
    for d in (4, -4):
        signal(vouch.at[1], at_z(turn(z, d, 16)))
    lax.fori_loop(4, 8, norm_rows, 0)

    chunks, keeps = [], []
    for s in range(4):
        row = []
        for i, d in enumerate(steps):
            cols = pl.ds(pl.multiple_of(turn(y, d) * 2048 + flips[s] * 512, 512), 512)
            row.append(send(normed.at[:, cols], xs.at[s, mine], tok_s.at[s * 3 + i], tok_r.at[s * 3 + i], y_peers[i]))
        cols = pl.ds(pl.multiple_of(y * 2048 + flips[s] * 512, 512), 512)
        keep = pltpu.make_async_copy(normed.at[:, cols], xs.at[s, mine], keep_sem.at[s])
        keep.start()
        keeps.append(keep)
        chunks.append(row)

    def sum_along(k):
        for copy in along[k]:
            copy.wait_recv()
        part[k] = lt[x, far[k]] + lr[0, k] + lr[1, k] + lr[2, k]
        if k == 0:
            pl.semaphore_wait(vouch.at[1], 2)
        if k < 3:
            return send(part.at[k], pr.at[k], far_s.at[k], far_r.at[k], at(zh=far[k]))

    def outer_update(copies):
        for copy in copies:
            copy.wait_recv()
        loads[4].wait()
        loads[5].wait()
        total = part[3] + pr[0] + pr[1] + pr[2]
        mean_delta = g[...] - total / 16.0
        new_momentum = outer_beta * m[...] + mean_delta
        new_global = g[...] - outer_rate * (mean_delta + outer_beta * new_momentum)
        ng_o[...] = new_global
        nm_o[...] = new_momentum
        nt[zl, c, zh, x] = new_global.astype(BF16)
        piece = nt.at[zl, c, zh, x]
        return [send(piece, piece, gat_s.at[k], gat_r.at[k], at(zh=far[k])) for k in range(3)]

    def columns(h):
        return pl.ds(2 * h, 2)

    def gather_z(copies):
        for copy in copies:
            copy.wait_recv()
        line, wide = [], [[], []]
        for h in range(2):
            piece = nt.at[zl, c, columns(h), x]
            for i in range(3):
                line.append(send(piece, piece, line_s.at[h * 3 + i], line_r.at[h * 3 + i], z_peers[i]))
        for h in range(2):
            piece = nt.at[zl, c, columns(h), x]
            for i in range(3):
                wide[h].append(send(piece, piece, wide_s.at[h * 12 + i], wide_r.at[h * 12 + i], x_peers[i]))
        return line, wide

    def gather_x(line, wide):
        for h in range(2):
            for j in range(3):
                line[h * 3 + j].wait_recv()
                piece = nt.at[z_from[j], c, columns(h), x]
                for i in range(3):
                    n = h * 12 + 3 + j * 3 + i
                    wide[h].append(send(piece, piece, wide_s.at[n], wide_r.at[n], x_peers[i]))

    def gather_core(wide, h):
        for copy in wide[h]:
            copy.wait_recv()
        piece = nt.at[:, c, columns(h)]
        return send(piece, piece, core_s.at[h], core_r.at[h], other)

    def half(core):
        return pl.ds(pl.multiple_of(core * 256, 256), 256)

    def grad_of(s, core):
        return lax.dot_general(
            xs[s, :, half(core)], cot[...], (((0,), (0,)), ((), ())), preferred_element_type=F32
        )

    def chunk_in(s):
        for copy in chunks[s]:
            copy.wait_recv()
        keeps[s].wait()
        gsend[s] = grad_of(s, 1 - c)
        copy = send(gsend.at[s], grecv.at[s], grad_s.at[s], grad_r.at[s], other)
        gown[s] = grad_of(s, c)
        return copy

    def arrived(slot):
        pltpu.make_async_remote_copy(
            src_ref=zsend.at[0], dst_ref=zrecv.at[slot], send_sem=z_s.at[0], recv_sem=z_r.at[slot],
            device_id=other, device_id_type=MESH,
        ).wait_recv()

    def chunk_out(s, copy):
        copy.wait_recv()
        total = gown[s] + grecv[s]
        if s == 0:
            zsend[s] = total.astype(BF16)
            slot = 3 * (1 - middle)
            owner = middle * flips[0] + (1 - middle) * flips[2]
            return send(zsend.at[s], zrecv.at[slot], z_s.at[s], z_r.at[slot], at(zl=owner))
        if s == 1:
            gown[s] = total

            @pl.when(middle == 1)
            def _():
                arrived(3)
                gown[s] = gown[s] + zrecv[3].astype(F32)

            total = gown[s]
        zsend[s] = total.astype(BF16)
        return send(zsend.at[s], zrecv.at[s], z_s.at[s], z_r.at[s], at(zl=flips[s]))

    def features(h):
        total = None
        for s in range(4):
            for core in range(2):
                rows = nt[flips[s], core, 2 * h:2 * h + 2].reshape(256, 256)
                term = lax.dot_general(
                    xs[s, :, core * 256:(core + 1) * 256], rows,
                    (((1,), (1,)), ((), ())), preferred_element_type=F32,
                )
                total = term if total is None else total + term
        for k in range(4):
            fown[h, k] = total[k * 128:(k + 1) * 128]
        out = []
        for i, d in enumerate(steps):
            fsend[h, i] = fown[h, turn(y, d)].astype(BF16)
            n = h * 3 + i
            out.append(send(fsend.at[h, i], frecv.at[h, i], feat_s.at[n], feat_r.at[n], y_peers[i]))
        return out

    far_copies = [sum_along(k) for k in range(4)][:3]
    for copy in cots:
        copy.wait_recv()
    gat_copies = outer_update(far_copies)
    g0 = chunk_in(0)
    line, wide = gather_z(gat_copies)
    chunk_out(0, g0)
    gather_x(line, wide)
    g1 = chunk_in(1)
    chunk_out(1, g1)
    g2 = chunk_in(2)
    core0 = gather_core(wide, 0)
    chunk_out(2, g2)
    core1 = gather_core(wide, 1)
    g3 = chunk_in(3)
    core0.wait_recv()
    feats = [features(0)]
    core1.wait_recv()
    feats.append(features(1))

    g3.wait_recv()
    for i in (6, 7, 8):
        loads[i].wait()
    arrived(1)
    arrived(2)
    gown[3] = gown[3] + grecv[3] + zrecv[1].astype(F32) + zrecv[2].astype(F32)

    @pl.when(middle == 1)
    def _():
        arrived(0)
        gown[3] = gown[3] + zrecv[0].astype(F32)

    grad = gown[3]
    first = beta_one * fm[...].astype(F32) + (1.0 - beta_one) * grad
    second = beta_two * sm[...].astype(F32) + (1.0 - beta_two) * grad * grad
    ratio = first / bias_first / (jnp.sqrt(second / bias_second) + adam_epsilon)
    w_o[...] = w[...] - inner_rate * (ratio + weight_decay * w[...])
    fm_o[...] = first.astype(BF16)
    sm_o[...] = second.astype(BF16)

    for h in range(2):
        for copy in feats[h]:
            copy.wait_recv()
        total = fown[h, y] + frecv[h, 0].astype(F32) + frecv[h, 1].astype(F32) + frecv[h, 2].astype(F32)
        ft_o[:, h * 256:(h + 1) * 256] = total.astype(BF16)

    for copy in sends:
        copy.wait_send()


def hand_over(*refs):
    for i in range(6):
        refs[6 + i][...] = refs[i][...]


def body(
    acts,
    norm_gain,
    cotangent,
    inner_weight,
    first_moment,
    second_moment,
    local_fragment,
    global_fragment,
    outer_momentum,
):
    vmem, anywhere = pl.BlockSpec(memory_space=pltpu.VMEM), pl.BlockSpec(memory_space=pl.ANY)
    dma = pltpu.SemaphoreType.DMA
    outs = pl.pallas_call(
        kernel,
        out_shape=(
            jax.ShapeDtypeStruct((256, 512), F32),
            jax.ShapeDtypeStruct((256, 512), BF16),
            jax.ShapeDtypeStruct((256, 512), BF16),
            jax.ShapeDtypeStruct((32, 256), F32),
            jax.ShapeDtypeStruct((32, 256), F32),
            jax.ShapeDtypeStruct((128, 512), BF16),
        ),
        in_specs=[anywhere] * 9,
        out_specs=[vmem] * 6,
        scratch_shapes=[
            pltpu.VMEM((128, 8192), BF16),
            pltpu.VMEM((1, 8192), F32),
            pltpu.VMEM((128, 8192), BF16),
            pltpu.VMEM((512, 512), BF16),
            pltpu.VMEM((256, 512), F32),
            pltpu.VMEM((256, 512), BF16),
            pltpu.VMEM((256, 512), BF16),
            pltpu.VMEM((256, 512), F32),
            pltpu.VMEM((32, 256), F32),
            pltpu.VMEM((32, 256), F32),
            pltpu.VMEM((4, 4, 32, 256), F32),
            pltpu.VMEM((3, 4, 32, 256), F32),
            pltpu.VMEM((4, 32, 256), F32),
            pltpu.VMEM((3, 32, 256), F32),
            pltpu.VMEM((4, 2, 4, 4, 32, 256), BF16),
            pltpu.VMEM((4, 512, 512), BF16),
            pltpu.VMEM((4, 256, 512), F32),
            pltpu.VMEM((4, 256, 512), F32),
            pltpu.VMEM((4, 256, 512), F32),
            pltpu.VMEM((3, 256, 512), BF16),
            pltpu.VMEM((4, 256, 512), BF16),
            pltpu.VMEM((2, 4, 128, 256), F32),
            pltpu.VMEM((2, 3, 128, 256), BF16),
            pltpu.VMEM((2, 3, 128, 256), BF16),
            dma((9,)), dma((4,)), pltpu.SemaphoreType.REGULAR((2,)),
        ] + [
            dma((n,)) for n in (3, 12, 12, 3, 3, 6, 24, 2, 4, 4, 6) for _ in range(2)
        ],
        compiler_params=pltpu.CompilerParams(
            collective_id=0, has_side_effects=True, vmem_limit_bytes=63 * 2**20
        ),
        name="window_step",
    )(
        acts, norm_gain[None], cotangent, inner_weight[0], first_moment[0], second_moment[0],
        local_fragment[0], global_fragment.T, outer_momentum.T,
    )
    outs = pl.pallas_call(
        hand_over,
        out_shape=[jax.ShapeDtypeStruct(out.shape, out.dtype) for out in outs],
        in_specs=[vmem] * 6,
        out_specs=[vmem] * 6,
        name="finish",
    )(*outs)
    new_weight, new_first, new_second, new_global, new_momentum, features = outs
    return (new_weight[None], new_first[None], new_second[None], new_global.T, new_momentum.T, features)


def solution(mesh):
    placed = (
        P(("replica", "fsdp"), None),
        P(),
        P(("replica", "fsdp"), None),
        P("replica", "fsdp", None),
        P("replica", "fsdp", None),
        P("replica", "fsdp", None),
        P("replica", "fsdp", None),
        P("fsdp", "replica"),
        P("fsdp", "replica"),
    )
    return jax.shard_map(
        body,
        mesh=mesh,
        in_specs=placed,
        out_specs=(
            P("replica", "fsdp", None),
            P("replica", "fsdp", None),
            P("replica", "fsdp", None),
            P("fsdp", "replica"),
            P("fsdp", "replica"),
            P(("replica", "fsdp"), None),
        ),
        check_vma=False,
    )
```

```python
import functools

import jax
import jax.numpy as jnp
from jax import lax
from jax.experimental import pallas as pl
from jax.experimental.pallas import tpu as pltpu
from jax.sharding import PartitionSpec as P

beta_one = 0.9
beta_two = 0.95
adam_epsilon = 1e-08
inner_rate = 0.01
weight_decay = 0.1
bias_first = 1.0 - 0.9**20
bias_second = 1.0 - 0.95**20
outer_rate = 0.7
outer_beta = 0.9
norm_epsilon = 1e-05

MESH = pl.DeviceIdType.MESH
F32 = jnp.float32
BF16 = jnp.bfloat16


def kernel(
    acts_h, gain_h, cot_h, w_h, fm_h, sm_h, lf_h, g_h, m_h,
    w_o, fm_o, sm_o, ng_o, nm_o, ft_o,
    acts, gain, normed, cot, w, fm, sm, lf, g, m,
    lt, lr, part, pr, nt, xs, gown, zsend, zrecv, fpart, fcore, fown, fsend, frecv,
    load_sem, keep_sem, vouch,
    cot_s, cot_r, tok_s, tok_r, along_s, along_r, far_s, far_r, gat_s, gat_r,
    line_s, line_r, wide_s, wide_r, core_s, core_r,
    z_s, z_r, feat_s, feat_r,
):
    rep = lax.axis_index("replica")
    fs = lax.axis_index("fsdp")
    zh, x = rep // 4, lax.rem(rep, 4)
    y, zl, c = fs // 8, lax.rem(fs // 2, 4), lax.rem(fs, 2)
    z = zh * 4 + zl

    def at(zh=zh, x=x, y=y, zl=zl, c=c):
        return (zh * 4 + x, y * 8 + zl * 2 + c)

    def at_z(zz):
        return at(zh=zz // 4, zl=lax.rem(zz, 4))

    def turn(value, step, size=4):
        return lax.rem(value + step + size, size)

    sends = []

    def send(src, dst, ss, rs, device):
        copy = pltpu.make_async_remote_copy(
            src_ref=src, dst_ref=dst, send_sem=ss, recv_sem=rs,
            device_id=device, device_id_type=MESH,
        )
        copy.start()
        sends.append(copy)
        return copy

    def signal(sem, device):
        pl.semaphore_signal(sem, inc=1, device_id=device, device_id_type=MESH)

    other = at(c=1 - c)
    steps = (1, 3, 2)
    x_peers = [at(x=turn(x, d)) for d in steps]
    y_peers = [at(y=turn(y, d)) for d in steps]
    flips = (3 - zl, turn(zl, 2), zl + 1 - 2 * lax.rem(zl, 2), zl)
    middle = (zl * (3 - zl)) // 2
    line_peers = [at(zl=flips[s]) for s in range(3)]
    skew = 2 - 4 * lax.rem(zl, 2)
    z_peers = [at_z(turn(z, 1, 16)), at_z(turn(z, -1, 16)), at_z(turn(z, skew, 16))]
    z_from = (turn(zl, -1), turn(zl, 1), turn(zl, 2))
    mine = pl.ds(pl.multiple_of(c * 512 + y * 128, 128), 128)
    takers = [(turn(y, d), core) for d in steps for core in (c, 1 - c)] + [(y, 1 - c)]

    loads = []
    for i, (src, dst) in enumerate((
        (lf_h, lf), (acts_h, acts), (gain_h, gain),
        (cot_h, cot.at[mine]),
        (g_h, g), (m_h, m), (w_h, w), (fm_h, fm), (sm_h, sm),
    )):
        copy = pltpu.make_async_copy(src, dst, load_sem.at[i])
        copy.start()
        loads.append(copy)

    barrier = pltpu.get_barrier_semaphore()
    near = [other] + x_peers + y_peers
    near += line_peers + [at(y=turn(y, d), c=1 - c) for d in steps]
    near += [at_z(turn(z, d, 16)) for d in (1, -1, 2, -2)]
    for device in near:
        signal(barrier, device)

    loads[0].wait()
    for k in range(4):
        turned = lf[:, k * 128:(k + 1) * 128].T
        for j in range(4):
            lt[j, k] = turned[j * 32:(j + 1) * 32]
    loads[3].wait()

    pl.semaphore_wait(barrier, len(near))

    for d in (2, -2):
        signal(vouch.at[0], at_z(turn(z, d, 16)))
    far = [turn(zh, d) for d in (2, 1, 3, 0)]
    along = []
    for k in range(4):
        along.append([
            send(lt.at[turn(x, d), far[k]], lr.at[i, k], along_s.at[k * 3 + i], along_r.at[k * 3 + i], x_peers[i])
            for i, d in enumerate(steps)
        ])
    cots = [send(cot.at[mine], cot.at[mine], cot_s.at[i], cot_r.at[i], y_peers[i]) for i in range(3)]
    loads[1].wait()
    loads[2].wait()

    def norm_rows(i, carry):
        rows = pl.ds(pl.multiple_of(i * 16, 16), 16)
        full = acts[rows, :].astype(F32)
        rstd = lax.rsqrt(jnp.sum(full * full, axis=1, keepdims=True) / 8192.0 + norm_epsilon)
        normed[rows, :] = (full * rstd * gain[...]).astype(BF16)
        return carry

    pl.semaphore_wait(vouch.at[0], 2)
    for d in (4, -4):
        signal(vouch.at[1], at_z(turn(z, d, 16)))
    lax.fori_loop(0, 8, norm_rows, 0)

    def columns_of(yy, s, core):
        return pl.ds(pl.multiple_of(yy * 2048 + flips[s] * 512 + core * 256, 256), 256)

    for s in range(4):
        pltpu.make_async_copy(normed.at[:, columns_of(y, s, c)], xs.at[s, mine], keep_sem.at[s]).start()
        for n, (yy, core) in enumerate(takers):
            send(
                normed.at[:, columns_of(yy, s, core)], xs.at[s, mine],
                tok_s.at[s * 7 + n], tok_r.at[s * 7 + n], at(y=yy, c=core),
            )

    def landed(ref, sem):
        pltpu.make_async_remote_copy(
            src_ref=ref, dst_ref=ref, send_sem=z_s.at[0], recv_sem=sem,
            device_id=other, device_id_type=MESH,
        ).wait_recv()

    def sum_along(k):
        for copy in along[k]:
            copy.wait_recv()
        part[k] = lt[x, far[k]] + lr[0, k] + lr[1, k] + lr[2, k]
        if k == 0:
            pl.semaphore_wait(vouch.at[1], 2)
        if k < 3:
            send(part.at[k], pr.at[k], far_s.at[k], far_r.at[k], at(zh=far[k]))

    def cot_to_core():
        for copy in cots:
            copy.wait_recv()
        whole = cot.at[pl.ds(pl.multiple_of(c * 512, 512), 512)]
        send(whole, whole, cot_s.at[3], cot_r.at[3], other)

    def outer_update():
        for k in range(3):
            landed(pr.at[k], far_r.at[k])
        loads[4].wait()
        loads[5].wait()
        total = part[3] + pr[0] + pr[1] + pr[2]
        mean_delta = g[...] - total / 16.0
        new_momentum = outer_beta * m[...] + mean_delta
        new_global = g[...] - outer_rate * (mean_delta + outer_beta * new_momentum)
        ng_o[...] = new_global
        nm_o[...] = new_momentum
        nt[zl, zh, x] = new_global.astype(BF16)
        piece = nt.at[zl, zh, x]
        for k in range(3):
            send(piece, piece, gat_s.at[k], gat_r.at[k], at(zh=far[k]))

    def gather_z():
        for k in range(3):
            landed(nt.at[zl, far[k], x], gat_r.at[k])
        for h in range(2):
            piece = nt.at[zl, pl.ds(2 * h, 2), x]
            for i in range(3):
                send(piece, piece, line_s.at[h * 3 + i], line_r.at[h * 3 + i], z_peers[i])
        for h in range(2):
            piece = nt.at[zl, pl.ds(2 * h, 2), x]
            for i in range(3):
                send(piece, piece, wide_s.at[h * 12 + i], wide_r.at[h * 12 + i], x_peers[i])

    def gather_x(h):
        for j in range(3):
            piece = nt.at[z_from[j], pl.ds(2 * h, 2), x]
            landed(piece, line_r.at[h * 3 + j])
            for i in range(3):
                n = h * 12 + 3 + j * 3 + i
                send(piece, piece, wide_s.at[n], wide_r.at[n], x_peers[i])

    def grads(s):
        if s == 0:
            landed(cot.at[pl.ds(pl.multiple_of(512 - c * 512, 512), 512)], cot_r.at[3])
        for n in range(7):
            landed(xs.at[s, mine], tok_r.at[s * 7 + n])
        pltpu.make_async_copy(normed.at[:, pl.ds(0, 256)], xs.at[s, mine], keep_sem.at[s]).wait()
        total = lax.dot_general(
            xs[s], cot[...], (((0,), (0,)), ((), ())), preferred_element_type=F32
        )
        if s == 0:
            zsend[s] = total.astype(BF16)
            slot = 3 * (1 - middle)
            owner = middle * flips[0] + (1 - middle) * flips[2]
            send(zsend.at[s], zrecv.at[slot], z_s.at[s], z_r.at[slot], at(zl=owner))
            return
        if s == 3:
            gown[...] = total
            return
        if s == 1:
            gown[...] = total

            @pl.when(middle == 1)
            def _():
                landed(zrecv.at[3], z_r.at[3])
                gown[...] = gown[...] + zrecv[3].astype(F32)

            total = gown[...]
        zsend[s] = total.astype(BF16)
        send(zsend.at[s], zrecv.at[s], z_s.at[s], z_r.at[s], line_peers[s])

    def features(h):
        for j in range(4):
            for i, d in enumerate(steps):
                piece = nt.at[zl if j == 0 else z_from[j - 1], pl.ds(2 * h, 2), turn(x, -d)]
                landed(piece, wide_r.at[h * 12 + j * 3 + i])
        total = None
        for s in range(4):
            rows = nt[flips[s], 2 * h:2 * h + 2].reshape(256, 256)
            term = lax.dot_general(
                xs[s], rows, (((1,), (1,)), ((), ())), preferred_element_type=F32
            )
            total = term if total is None else total + term
        for k in range(8):
            fpart[h, k // 4, k % 4] = total[k * 128:(k + 1) * 128]
        fcore[h, 0] = fpart[h, 1 - c].astype(BF16)
        send(fcore.at[h, 0], fcore.at[h, 1], core_s.at[h], core_r.at[h], other)

    def features_along(h):
        landed(fcore.at[h, 1], core_r.at[h])
        fown[h] = fpart[h, c] + fcore[h, 1].astype(F32)
        for i, d in enumerate(steps):
            fsend[h, i] = fown[h, turn(y, d)].astype(BF16)
            n = h * 3 + i
            send(fsend.at[h, i], frecv.at[h, i], feat_s.at[n], feat_r.at[n], y_peers[i])

    def inner_update():
        for i in (6, 7, 8):
            loads[i].wait()
        landed(zrecv.at[1], z_r.at[1])
        landed(zrecv.at[2], z_r.at[2])
        gown[...] = gown[...] + zrecv[1].astype(F32) + zrecv[2].astype(F32)

        @pl.when(middle == 1)
        def _():
            landed(zrecv.at[0], z_r.at[0])
            gown[...] = gown[...] + zrecv[0].astype(F32)

        grad = gown[...]
        first = beta_one * fm[...].astype(F32) + (1.0 - beta_one) * grad
        second = beta_two * sm[...].astype(F32) + (1.0 - beta_two) * grad * grad
        ratio = first / bias_first / (jnp.sqrt(second / bias_second) + adam_epsilon)
        w_o[...] = w[...] - inner_rate * (ratio + weight_decay * w[...])
        fm_o[...] = first.astype(BF16)
        sm_o[...] = second.astype(BF16)

    def features_out(h):
        total = fown[h, y]
        for i in range(3):
            landed(frecv.at[h, i], feat_r.at[h * 3 + i])
            total = total + frecv[h, i].astype(F32)
        ft_o[:, h * 256:(h + 1) * 256] = total.astype(BF16)

    for k in range(4):
        sum_along(k)
    cot_to_core()
    outer_update()
    grads(0)
    gather_z()
    gather_x(0)
    gather_x(1)
    grads(1)
    grads(2)
    grads(3)
    features(0)
    features_along(0)
    features(1)
    features_along(1)
    inner_update()
    features_out(0)
    features_out(1)

    for copy in sends:
        copy.wait_send()


def hand_over(*refs):
    copies = []
    for i in range(6):
        copy = pltpu.make_async_copy(refs[i], refs[6 + i], refs[12].at[i])
        copy.start()
        copies.append(copy)
    for copy in copies:
        copy.wait()


def body(
    acts,
    norm_gain,
    cotangent,
    inner_weight,
    first_moment,
    second_moment,
    local_fragment,
    global_fragment,
    outer_momentum,
):
    vmem, anywhere = pl.BlockSpec(memory_space=pltpu.VMEM), pl.BlockSpec(memory_space=pl.ANY)
    dma = pltpu.SemaphoreType.DMA
    outs = pl.pallas_call(
        kernel,
        out_shape=(
            pltpu.VMEM((256, 512), F32),
            pltpu.VMEM((256, 512), BF16),
            pltpu.VMEM((256, 512), BF16),
            pltpu.VMEM((32, 256), F32),
            pltpu.VMEM((32, 256), F32),
            pltpu.VMEM((128, 512), BF16),
        ),
        in_specs=[anywhere] * 9,
        out_specs=[vmem] * 6,
        scratch_shapes=[
            pltpu.VMEM((128, 8192), BF16),
            pltpu.VMEM((1, 8192), F32),
            pltpu.VMEM((128, 8192), BF16),
            pltpu.VMEM((1024, 512), BF16),
            pltpu.VMEM((256, 512), F32),
            pltpu.VMEM((256, 512), BF16),
            pltpu.VMEM((256, 512), BF16),
            pltpu.VMEM((256, 512), F32),
            pltpu.VMEM((32, 256), F32),
            pltpu.VMEM((32, 256), F32),
            pltpu.VMEM((4, 4, 32, 256), F32),
            pltpu.VMEM((3, 4, 32, 256), F32),
            pltpu.VMEM((4, 32, 256), F32),
            pltpu.VMEM((3, 32, 256), F32),
            pltpu.VMEM((4, 4, 4, 32, 256), BF16),
            pltpu.VMEM((4, 1024, 256), BF16),
            pltpu.VMEM((256, 512), F32),
            pltpu.VMEM((3, 256, 512), BF16),
            pltpu.VMEM((4, 256, 512), BF16),
            pltpu.VMEM((2, 2, 4, 128, 256), F32),
            pltpu.VMEM((2, 2, 4, 128, 256), BF16),
            pltpu.VMEM((2, 4, 128, 256), F32),
            pltpu.VMEM((2, 3, 128, 256), BF16),
            pltpu.VMEM((2, 3, 128, 256), BF16),
            dma((9,)), dma((4,)), pltpu.SemaphoreType.REGULAR((2,)),
        ] + [
            dma((n,)) for n in (4, 28, 12, 3, 3, 6, 24, 2, 4, 6) for _ in range(2)
        ],
        compiler_params=pltpu.CompilerParams(
            collective_id=0, has_side_effects=True, vmem_limit_bytes=60 * 2**20
        ),
        name="window_step",
    )(
        acts, norm_gain[None], cotangent, inner_weight[0], first_moment[0], second_moment[0],
        local_fragment[0], global_fragment.T, outer_momentum.T,
    )
    outs = pl.pallas_call(
        hand_over,
        out_shape=[jax.ShapeDtypeStruct(out.shape, out.dtype) for out in outs],
        in_specs=[anywhere] * 6,
        out_specs=[anywhere] * 6,
        scratch_shapes=[dma((6,))],
        name="finish",
    )(*[pltpu.with_memory_space_constraint(out, pltpu.VMEM) for out in outs])
    new_weight, new_first, new_second, new_global, new_momentum, features = outs
    return (new_weight[None], new_first[None], new_second[None], new_global.T, new_momentum.T, features)


def solution(mesh):
    placed = (
        P(("replica", "fsdp"), None),
        P(),
        P(("replica", "fsdp"), None),
        P("replica", "fsdp", None),
        P("replica", "fsdp", None),
        P("replica", "fsdp", None),
        P("replica", "fsdp", None),
        P("fsdp", "replica"),
        P("fsdp", "replica"),
    )
    return jax.shard_map(
        body,
        mesh=mesh,
        in_specs=placed,
        out_specs=(
            P("replica", "fsdp", None),
            P("replica", "fsdp", None),
            P("replica", "fsdp", None),
            P("fsdp", "replica"),
            P("fsdp", "replica"),
            P(("replica", "fsdp"), None),
        ),
        check_vma=False,
    )
```
